32 devices in a mesh: dp: 4 (over x, core), ctx: 8 (over z, y).
Axes of the slice: x: 2, y: 2, z: 4, core: 2. Of those that a mesh axis runs over, the one named last changes fastest.
Arguments:
- queries: bfloat16 [4, 1024, 2048], P('dp', 'ctx'), may hold values from -6 to 6
- keys: bfloat16 [4, 1024, 2048], P('dp', 'ctx'), may hold values from -6 to 6
- values: bfloat16 [4, 1024, 2048], P('dp', 'ctx'), may hold values from -6 to 6
- cotangent: bfloat16 [4, 1024, 2048], P('dp', 'ctx'), may hold values from -6 to 6
- doc_lengths: int32 [4, 4], P('dp'), may hold values from 0 to 1024, as said below
- filter_taps: float32 [1024, 2048], P('ctx'), may hold values from -0.1875 to 0.1875
Outputs:
- hyena_out: bfloat16 [4, 1024, 2048], P('dp', 'ctx')
- grad_queries: bfloat16 [4, 1024, 2048], P('dp', 'ctx')
- grad_keys: bfloat16 [4, 1024, 2048], P('dp', 'ctx')
- grad_values: bfloat16 [4, 1024, 2048], P('dp', 'ctx')
- grad_filter: float32 [1024, 2048], P('ctx', 'dp')
The draws below stay inside these ranges and needn't reach their ends.
Inputs may be any that keep to these rules, and one draw needn't show every extreme that they name: `doc_lengths`: each row holds 4 document lengths that sum to 1024; a length may be zero (an unused slot); in every draw some row holds a single document of all 1024 positions.
All inputs are finite; a program needn't handle non-finite values.
Results may differ from the reference program's by a relative error of at most 0.0051.
Values may be sent and summed in bfloat16 or wider, within the bound.
A program may use at most 512 MiB of HBM per device.

```python
import jax
import jax.numpy as jnp
from jax import lax

D = 2048
DOCS = 4
SEQ = 1024
BATCH = 4


def draw_doc_lengths(key, part):
    cut_key = jax.random.fold_in(key, 11)
    row_key = jax.random.fold_in(key, 23)
    cut_points = jnp.sort(jax.random.randint(cut_key, (BATCH, DOCS - 1), 0, SEQ + 1), axis=1).astype(jnp.int32)
    whole_row = jax.random.randint(row_key, (), 0, BATCH).astype(jnp.int32)
    row_index = lax.broadcasted_iota(jnp.int32, (BATCH, DOCS - 1), 0)
    cut_points = jnp.where(row_index == whole_row, SEQ, cut_points).astype(jnp.int32)
    bounds = jnp.concatenate([jnp.zeros((BATCH, 1), jnp.int32), cut_points, jnp.full((BATCH, 1), SEQ, jnp.int32)], axis=1)
    return (bounds[:, 1:] - bounds[:, :-1]).astype(jnp.int32)


def with_spikes(drawn, key, source, target, shards_of, factor):
    def block_of(axis_at):
        return (jnp.arange(drawn.shape[axis_at]) // (drawn.shape[axis_at] // shards_of)).reshape((-1,) + (1,) * (drawn.ndim - 1 - axis_at))

    first = jax.random.permutation(key, shards_of)[block_of(target)]
    second = (block_of(target) + shards_of // 2) % shards_of
    return jnp.where((block_of(source) == first) | (block_of(source) == second), factor * drawn, drawn)


def block_scale(key, dims, cuts, low, top_value):
    loudness, own = 1.0, jax.random.fold_in(key, 6)
    for axis_at, parts in cuts:
        steps = jnp.exp(jax.random.uniform(jax.random.fold_in(own, axis_at), (parts,), jnp.float32, low / len(cuts), top_value / len(cuts)))
        loudness = loudness * jnp.repeat(steps, dims[axis_at] // parts).reshape([-1 if axis == axis_at else 1 for axis in range(len(dims))])
    return loudness


def scatter_about(rng, dims, deviation, reach, shards=(), kind=jnp.bfloat16):
    loudness = block_scale(rng, dims, shards, -0.22, 0.18) if shards else 1.0
    values = jax.random.normal(rng, dims, jnp.float32) * deviation * loudness
    return jnp.minimum(jnp.maximum(values, -reach), reach).astype(kind)


def heavy_noise(rng, extent, spread, limit, split, heavy, kind=jnp.bfloat16):
    values = spread * jax.random.normal(rng, extent, jnp.float32)
    if split:
        values = values * block_scale(rng, extent, split, -0.22, 0.18)
    return jnp.clip(with_spikes(values, jax.random.fold_in(rng, 3), *heavy), -limit, limit).astype(kind)


def setup_inputs(seed: int = 0) -> dict:
    seeds = jax.random.split(jax.random.key(seed), 7)
    return {
        "queries": scatter_about(seeds[0], (BATCH, SEQ, D), 1.0, 6.0, ((0, 4), (1, 8))),
        "keys": scatter_about(seeds[1], (BATCH, SEQ, D), 1.0, 6.0, ((0, 4), (1, 8))),
        "values": scatter_about(seeds[2], (BATCH, SEQ, D), 1.0, 6.0, ((0, 4), (1, 8))),
        "cotangent": heavy_noise(seeds[3], (BATCH, SEQ, D), 1.0, 6.0, ((0, 4), (1, 8)), (0, 2, 4, 2.0)),
        "doc_lengths": draw_doc_lengths(jax.random.fold_in(seeds[6], 71), 0),
        "filter_taps": scatter_about(seeds[5], (SEQ, D), (SEQ ** -0.5), 0.1875, ((0, 8),), jnp.float32),
    }


def document_ids(lengths, count):
    doc_ends = jnp.cumsum(lengths)
    positions = jnp.arange(count, dtype=jnp.int32)
    return lax.optimization_barrier(jnp.sum((doc_ends[None, :] <= positions[:, None]).astype(jnp.int32), axis=1))

def reset_convolution(filter_taps, signal, doc_of):
    period = 2 * signal.shape[0]
    filter_freq = jnp.fft.rfft(filter_taps, period, axis=0)
    total = jnp.zeros_like(signal)
    for doc_index in range(DOCS):
        keep_col = (doc_of == doc_index).astype(signal.dtype)[:, None]
        spectrum = filter_freq * jnp.fft.rfft(keep_col * signal, period, axis=0)
        part_conv = jnp.fft.irfft(spectrum, period, axis=0)[:signal.shape[0]]
        total = total + keep_col * part_conv
    return total

def reference(queries, keys, values, cotangent, doc_lengths, filter_taps):

    def one_sequence(grad_sum, inputs):
        query_row, key_row, value_row, cot_row, length_row = inputs
        doc_of = document_ids(length_row, SEQ)
        query_f = query_row.astype(jnp.float32)
        key_f = key_row.astype(jnp.float32)
        value_f = value_row.astype(jnp.float32)
        cot_f = cot_row.astype(jnp.float32)
        gated = lax.optimization_barrier((key_f * value_f).astype(jnp.bfloat16)).astype(jnp.float32)
        conv_out, pullback = jax.vjp(lambda taps, signal: reset_convolution(taps, signal, doc_of), filter_taps, gated)
        weighted = lax.optimization_barrier((cot_f * query_f).astype(jnp.bfloat16)).astype(jnp.float32)
        grad_taps, grad_signal = pullback(weighted)
        outputs = ((query_f * conv_out).astype(jnp.bfloat16), (cot_f * conv_out).astype(jnp.bfloat16), (grad_signal * value_f).astype(jnp.bfloat16), (grad_signal * key_f).astype(jnp.bfloat16))
        return (grad_sum + grad_taps, outputs)
    grad_total, outputs = lax.scan(one_sequence, jnp.zeros_like(filter_taps), (queries, keys, values, cotangent, doc_lengths))
    return (outputs[0], outputs[1], outputs[2], outputs[3], grad_total)
```

```python
import functools
import math

import jax
import jax.numpy as jnp
import numpy as np
import ml_dtypes
from jax import lax
from jax.experimental import pallas as pl
from jax.experimental.pallas import tpu as pltpu
from jax.sharding import PartitionSpec as P


def tables(block_len):
    turns = (2 * np.arange(block_len)[:, None] + 1) * np.arange(block_len)[None, :]
    angle = (turns % (4 * block_len)) * (2.0 * math.pi / (4 * block_len))
    forward = np.concatenate([np.cos(angle), -np.sin(angle)], axis=0)
    inverse = forward.T / block_len

    def split(table):
        high = table.astype(ml_dtypes.bfloat16)
        low = (table - high.astype(np.float64)).astype(ml_dtypes.bfloat16)
        return high, low

    fwd_high, fwd_low = split(forward)
    inv_high, inv_low = split(inverse)
    return (
        np.concatenate([fwd_high, fwd_low], axis=1),
        np.concatenate([inv_high, inv_high, inv_low], axis=1),
    )


def conv_kernel(
    lengths_ref, rows_ref, fwd_ref, inv_ref, conv_ref, lag_ref,
    in_spec, wt_spec, filt_spec, conv_spec, adj_spec, lag_spec, conv_acc, adj_acc,
):
    blocks, double, channels = in_spec.shape
    block_len = double // 2
    docs = lengths_ref.shape[1]
    row_id = lax.broadcasted_iota(jnp.int32, (block_len, channels), 0)
    sign = (1 - 2 * (row_id % 2)).astype(jnp.float32)
    chunk = 16

    def rows_at(block):
        return pl.ds(pl.multiple_of(block * block_len, block_len), block_len)

    def forward(rows):
        return jnp.dot(
            fwd_ref[...], jnp.concatenate([rows, rows], axis=0), preferred_element_type=jnp.float32
        )

    def inverse(spec):
        high = spec.astype(jnp.bfloat16)
        low = (spec - high.astype(jnp.float32)).astype(jnp.bfloat16)
        return jnp.dot(
            inv_ref[...], jnp.concatenate([high, low, high], axis=0),
            preferred_element_type=jnp.float32,
        )

    @pl.loop(0, blocks)
    def _(block):
        adj_spec[block] = forward(rows_ref[2, rows_at(block), :])
        lag_spec[block] = jnp.zeros((double, channels), jnp.float32)

    filt_spec[0] = adj_spec[0]

    @pl.loop(1, blocks)
    def _(block):
        filt_spec[block, :block_len] = (
            adj_spec[block, :block_len] - sign * adj_spec[block - 1, block_len:]
        )
        filt_spec[block, block_len:] = (
            adj_spec[block, block_len:] + sign * adj_spec[block - 1, :block_len]
        )

    conv_acc[...] = jnp.zeros_like(conv_acc)
    adj_acc[...] = jnp.zeros_like(adj_acc)

    def doc_work(doc, start):
        length = lengths_ref[0, doc]
        end = start + length
        low_block = start // block_len
        high_block = jnp.where(length > 0, (end + block_len - 1) // block_len, low_block)

        def keep(block):
            pos = row_id + block * block_len
            return (pos >= start) & (pos < end)

        @pl.loop(low_block, high_block)
        def _(block):
            kept = keep(block)

            def masked(which):
                rows = rows_ref[which, rows_at(block), :].astype(jnp.float32)
                return jnp.where(kept, rows, 0.0).astype(jnp.bfloat16)

            in_spec[block] = forward(masked(0))
            wt_spec[block] = forward(masked(1))
            conv_spec[block] = jnp.zeros((double, channels), jnp.float32)
            adj_spec[block] = jnp.zeros((double, channels), jnp.float32)

        @pl.loop(low_block, high_block)
        def _(target):
            @pl.loop(low_block, target + 1)
            def _(source):
                lag = target - source
                for base in range(0, block_len, chunk):
                    re = pl.ds(base, chunk)
                    im = pl.ds(base + block_len, chunk)
                    filt_re, filt_im = filt_spec[lag, re], filt_spec[lag, im]
                    in_re, in_im = in_spec[source, re], in_spec[source, im]
                    wt_re, wt_im = wt_spec[target, re], wt_spec[target, im]
                    conv_spec[target, re] += filt_re * in_re - filt_im * in_im
                    conv_spec[target, im] += filt_re * in_im + filt_im * in_re
                    adj_spec[source, re] += filt_re * wt_re + filt_im * wt_im
                    adj_spec[source, im] += filt_re * wt_im - filt_im * wt_re
                    lag_spec[lag, re] += wt_re * in_re + wt_im * in_im
                    lag_spec[lag, im] += wt_im * in_re - wt_re * in_im

        @pl.loop(low_block, high_block)
        def _(block):
            kept = keep(block)
            conv_acc[rows_at(block), :] += jnp.where(kept, inverse(conv_spec[block]), 0.0)
            adj_acc[rows_at(block), :] += jnp.where(kept, inverse(adj_spec[block]), 0.0)

        return end

    lax.fori_loop(0, docs, doc_work, jnp.int32(0))
    conv_ref[0] = conv_acc[...].astype(jnp.bfloat16)
    conv_ref[1] = adj_acc[...].astype(jnp.bfloat16)

    @pl.loop(0, blocks - 1)
    def _(block):
        real = lag_spec[block, :block_len] + sign * lag_spec[block + 1, block_len:]
        imag = lag_spec[block, block_len:] - sign * lag_spec[block + 1, :block_len]
        lag_ref[rows_at(block), :] = inverse(jnp.concatenate([real, imag], axis=0))

    lag_ref[rows_at(blocks - 1), :] = inverse(lag_spec[blocks - 1])


def local_conv(lengths, rows, block_len):
    _, seq, channels = rows.shape
    blocks = seq // block_len
    fwd_table, inv_table = tables(block_len)
    spec = pltpu.VMEM((blocks, 2 * block_len, channels), jnp.float32)
    vmem = pl.BlockSpec(memory_space=pltpu.VMEM)
    return pl.pallas_call(
        conv_kernel,
        out_shape=(
            jax.ShapeDtypeStruct((2, seq, channels), jnp.bfloat16),
            jax.ShapeDtypeStruct((seq, channels), jnp.float32),
        ),
        in_specs=[pl.BlockSpec(memory_space=pltpu.SMEM), vmem, vmem, vmem],
        out_specs=(vmem, vmem),
        scratch_shapes=[spec] * 6 + [pltpu.VMEM((seq, channels), jnp.float32)] * 2,
        compiler_params=pltpu.CompilerParams(vmem_limit_bytes=40 * 1024 * 1024),
    )(lengths, rows, jnp.asarray(fwd_table), jnp.asarray(inv_table))


def body(queries, keys, values, cotangent, doc_lengths, filter_taps):
    block_len = queries.shape[1]
    ctx_size = lax.axis_size("ctx")
    dp_size = lax.axis_size("dp")
    ratio = ctx_size // dp_size
    ctx_rank = lax.axis_index("ctx")
    query_f = queries[0].astype(jnp.float32)
    key_f = keys[0].astype(jnp.float32)
    value_f = values[0].astype(jnp.float32)
    cot_f = cotangent[0].astype(jnp.float32)
    gated = (key_f * value_f).astype(jnp.bfloat16)
    weighted = (cot_f * query_f).astype(jnp.bfloat16)
    packed = jnp.stack([gated, weighted, filter_taps.astype(jnp.bfloat16)])
    rows = lax.all_to_all(packed, "ctx", split_axis=2, concat_axis=1, tiled=True)
    both, lags = local_conv(doc_lengths, rows, block_len)
    back = lax.all_to_all(both, "ctx", split_axis=1, concat_axis=2, tiled=True)
    lag_share = lax.psum_scatter(lags, "dp", scatter_dimension=0, tiled=True)
    lag_share = lag_share.reshape(ratio, block_len, -1)
    arrived = []
    for step in range(ratio):
        pairs = [
            (d * ctx_size + c, (c // ratio) * ctx_size + ratio * d + (c + step) % ratio)
            for d in range(dp_size)
            for c in range(ctx_size)
        ]
        piece = lax.dynamic_index_in_dim(lag_share, (ctx_rank + step) % ratio, 0, keepdims=False)
        arrived.append(lax.ppermute(piece, ("dp", "ctx"), pairs))
    arrived = jnp.stack(arrived)
    grad_filter = jnp.concatenate(
        [
            lax.dynamic_index_in_dim(arrived, (ctx_rank - m) % ratio, 0, keepdims=False)
            for m in range(ratio)
        ],
        axis=1,
    )
    conv_rows = back[0].astype(jnp.float32)
    adj_rows = back[1].astype(jnp.float32)
    hyena_out = (query_f * conv_rows).astype(jnp.bfloat16)
    grad_queries = (cot_f * conv_rows).astype(jnp.bfloat16)
    grad_keys = (adj_rows * value_f).astype(jnp.bfloat16)
    grad_values = (adj_rows * key_f).astype(jnp.bfloat16)
    return (hyena_out[None], grad_queries[None], grad_keys[None], grad_values[None], grad_filter)


def solution(mesh):
    in_specs = (
        P("dp", "ctx", None),
        P("dp", "ctx", None),
        P("dp", "ctx", None),
        P("dp", "ctx", None),
        P("dp", None),
        P("ctx", None),
    )
    out_specs = (
        P("dp", "ctx", None),
        P("dp", "ctx", None),
        P("dp", "ctx", None),
        P("dp", "ctx", None),
        P("ctx", "dp"),
    )
    return jax.shard_map(body, mesh=mesh, in_specs=in_specs, out_specs=out_specs, check_vma=False)
```

```python
import functools
import math

import jax
import jax.numpy as jnp
import numpy as np
import ml_dtypes
from jax import lax
from jax.experimental import pallas as pl
from jax.experimental.pallas import tpu as pltpu
from jax.sharding import PartitionSpec as P


def tables(block_len):
    turns = (2 * np.arange(block_len)[:, None] + 1) * np.arange(block_len)[None, :]
    angle = (turns % (4 * block_len)) * (2.0 * math.pi / (4 * block_len))
    forward = np.concatenate([np.cos(angle), -np.sin(angle)], axis=0)
    inverse = forward.T / block_len

    def split(table):
        high = table.astype(ml_dtypes.bfloat16)
        low = (table - high.astype(np.float64)).astype(ml_dtypes.bfloat16)
        return high, low

    fwd_high, fwd_low = split(forward)
    inv_high, inv_low = split(inverse)
    return (
        np.concatenate([fwd_high, fwd_low], axis=1),
        np.concatenate([inv_high, inv_high, inv_low], axis=1),
    )


def conv_kernel(
    lengths_ref, rows_ref, taps_ref, fwd_ref, inv_ref, conv_ref, lag_ref,
    in_spec, wt_spec, filt_spec, conv_spec, adj_spec, lag_spec, conv_acc, adj_acc,
):
    blocks, double, channels = in_spec.shape
    block_len = double // 2
    docs = lengths_ref.shape[1]
    row_id = lax.broadcasted_iota(jnp.int32, (block_len, channels), 0)
    sign = (1 - 2 * (row_id % 2)).astype(jnp.float32)
    chunk = 16

    def rows_at(block):
        return pl.ds(pl.multiple_of(block * block_len, block_len), block_len)

    def forward(rows):
        return jnp.dot(
            fwd_ref[...], jnp.concatenate([rows, rows], axis=0), preferred_element_type=jnp.float32
        )

    def inverse(spec):
        high = spec.astype(jnp.bfloat16)
        low = (spec - high.astype(jnp.float32)).astype(jnp.bfloat16)
        return jnp.dot(
            inv_ref[...], jnp.concatenate([high, low, high], axis=0),
            preferred_element_type=jnp.float32,
        )

    @pl.loop(0, blocks)
    def _(block):
        taps = [taps_ref[part, block] for part in range(taps_ref.shape[0])]
        adj_spec[block] = forward(jnp.concatenate(taps, axis=0))
        lag_spec[block] = jnp.zeros((double, channels), jnp.float32)

    filt_spec[0] = adj_spec[0]

    @pl.loop(1, blocks)
    def _(block):
        filt_spec[block, :block_len] = (
            adj_spec[block, :block_len] - sign * adj_spec[block - 1, block_len:]
        )
        filt_spec[block, block_len:] = (
            adj_spec[block, block_len:] + sign * adj_spec[block - 1, :block_len]
        )

    conv_acc[...] = jnp.zeros_like(conv_acc)
    adj_acc[...] = jnp.zeros_like(adj_acc)

    def doc_work(doc, start):
        length = lengths_ref[0, doc]
        end = start + length
        low_block = start // block_len
        high_block = jnp.where(length > 0, (end + block_len - 1) // block_len, low_block)

        def keep(block):
            pos = row_id + block * block_len
            return (pos >= start) & (pos < end)

        @pl.loop(low_block, high_block)
        def _(block):
            kept = keep(block)

            def masked(which):
                rows = rows_ref[block, which].astype(jnp.float32)
                return jnp.where(kept, rows, 0.0).astype(jnp.bfloat16)

            in_spec[block] = forward(masked(0))
            wt_spec[block] = forward(masked(1))
            conv_spec[block] = jnp.zeros((double, channels), jnp.float32)
            adj_spec[block] = jnp.zeros((double, channels), jnp.float32)

        @pl.loop(low_block, high_block)
        def _(target):
            @pl.loop(low_block, target + 1)
            def _(source):
                lag = target - source
                for base in range(0, block_len, chunk):
                    re = pl.ds(base, chunk)
                    im = pl.ds(base + block_len, chunk)
                    filt_re, filt_im = filt_spec[lag, re], filt_spec[lag, im]
                    in_re, in_im = in_spec[source, re], in_spec[source, im]
                    wt_re, wt_im = wt_spec[target, re], wt_spec[target, im]
                    conv_spec[target, re] += filt_re * in_re - filt_im * in_im
                    conv_spec[target, im] += filt_re * in_im + filt_im * in_re
                    adj_spec[source, re] += filt_re * wt_re + filt_im * wt_im
                    adj_spec[source, im] += filt_re * wt_im - filt_im * wt_re
                    lag_spec[lag, re] += wt_re * in_re + wt_im * in_im
                    lag_spec[lag, im] += wt_im * in_re - wt_re * in_im

        @pl.loop(low_block, high_block)
        def _(block):
            kept = keep(block)
            conv_acc[rows_at(block), :] += jnp.where(kept, inverse(conv_spec[block]), 0.0)
            adj_acc[rows_at(block), :] += jnp.where(kept, inverse(adj_spec[block]), 0.0)

        return end

    lax.fori_loop(0, docs, doc_work, jnp.int32(0))

    @pl.loop(0, blocks)
    def _(block):
        conv_ref[block, 0] = conv_acc[rows_at(block), :].astype(jnp.bfloat16)
        conv_ref[block, 1] = adj_acc[rows_at(block), :].astype(jnp.bfloat16)

    @pl.loop(0, blocks - 1)
    def _(block):
        real = lag_spec[block, :block_len] + sign * lag_spec[block + 1, block_len:]
        imag = lag_spec[block, block_len:] - sign * lag_spec[block + 1, :block_len]
        lag_ref[rows_at(block), :] = inverse(jnp.concatenate([real, imag], axis=0))

    lag_ref[rows_at(blocks - 1), :] = inverse(lag_spec[blocks - 1])


def local_conv(lengths, rows, taps):
    blocks, _, block_len, channels = rows.shape
    seq = blocks * block_len
    fwd_table, inv_table = tables(block_len)
    spec = pltpu.VMEM((blocks, 2 * block_len, channels), jnp.float32)
    vmem = pl.BlockSpec(memory_space=pltpu.VMEM)
    return pl.pallas_call(
        conv_kernel,
        out_shape=(
            jax.ShapeDtypeStruct(rows.shape, jnp.bfloat16),
            jax.ShapeDtypeStruct((seq, channels), jnp.float32),
        ),
        in_specs=[pl.BlockSpec(memory_space=pltpu.SMEM), vmem, vmem, vmem, vmem],
        out_specs=(vmem, vmem),
        scratch_shapes=[spec] * 6 + [pltpu.VMEM((seq, channels), jnp.float32)] * 2,
        compiler_params=pltpu.CompilerParams(vmem_limit_bytes=40 * 1024 * 1024),
    )(lengths, rows, taps, jnp.asarray(fwd_table), jnp.asarray(inv_table))


GROUP = 2


def gate_kernel(query_ref, key_ref, value_ref, cot_ref, out_ref):
    channels = out_ref.shape[3]
    for part in range(GROUP):
        cols = pl.ds(part * channels, channels)

        def load(ref):
            return ref[0, :, cols].astype(jnp.float32)

        out_ref[part, 0] = (load(key_ref) * load(value_ref)).astype(jnp.bfloat16)
        out_ref[part, 1] = (load(cot_ref) * load(query_ref)).astype(jnp.bfloat16)


def finish_kernel(
    back_ref, query_ref, key_ref, value_ref, cot_ref, out_ref, dquery_ref, dkey_ref, dvalue_ref
):
    channels = back_ref.shape[3]
    for part in range(GROUP):
        cols = pl.ds(part * channels, channels)

        def load(ref):
            return ref[0, :, cols].astype(jnp.float32)

        conv_rows = back_ref[part, 0].astype(jnp.float32)
        adj_rows = back_ref[part, 1].astype(jnp.float32)
        out_ref[0, :, cols] = (load(query_ref) * conv_rows).astype(jnp.bfloat16)
        dquery_ref[0, :, cols] = (load(cot_ref) * conv_rows).astype(jnp.bfloat16)
        dkey_ref[0, :, cols] = (adj_rows * load(value_ref)).astype(jnp.bfloat16)
        dvalue_ref[0, :, cols] = (adj_rows * load(key_ref)).astype(jnp.bfloat16)


def body(queries, keys, values, cotangent, doc_lengths, filter_taps):
    block_len, width = queries.shape[1:]
    ctx_size = lax.axis_size("ctx")
    dp_size = lax.axis_size("dp")
    ratio = ctx_size // dp_size
    ctx_rank = lax.axis_index("ctx")
    channels = width // ctx_size
    wide = pl.BlockSpec((1, block_len, GROUP * channels), lambda i: (0, 0, i))
    packed_spec = pl.BlockSpec((GROUP, 2, block_len, channels), lambda i: (i, 0, 0, 0))
    share = block_len // dp_size
    piece = lax.dynamic_slice_in_dim(filter_taps, lax.axis_index("dp") * share, share, 0)
    piece = piece.astype(jnp.bfloat16).reshape(share, ctx_size, channels).transpose(1, 0, 2)
    piece = lax.all_to_all(piece, "ctx", split_axis=0, concat_axis=0, tiled=True)
    packed = pl.pallas_call(
        gate_kernel,
        grid=(ctx_size // GROUP,),
        out_shape=jax.ShapeDtypeStruct((ctx_size, 2, block_len, channels), jnp.bfloat16),
        in_specs=[wide] * 4,
        out_specs=packed_spec,
    )(queries, keys, values, cotangent)
    packed, piece = lax.optimization_barrier((packed, piece))
    taps = lax.all_gather(piece, "dp", axis=0, tiled=False)
    rows = lax.all_to_all(packed, "ctx", split_axis=0, concat_axis=0, tiled=True)
    both, lags = local_conv(doc_lengths, rows, taps)
    back = lax.all_to_all(both, "ctx", split_axis=0, concat_axis=0, tiled=True)
    lag_share = lax.psum_scatter(lags, "dp", scatter_dimension=0, tiled=True)
    lag_share = lag_share.reshape(ratio, block_len, -1)
    arrived = []
    for step in range(ratio):
        pairs = [
            (d * ctx_size + c, (c // ratio) * ctx_size + ratio * d + (c + step) % ratio)
            for d in range(dp_size)
            for c in range(ctx_size)
        ]
        piece = lax.dynamic_index_in_dim(lag_share, (ctx_rank + step) % ratio, 0, keepdims=False)
        arrived.append(lax.ppermute(piece, ("dp", "ctx"), pairs))
    arrived = jnp.stack(arrived)
    grad_filter = jnp.concatenate(
        [
            lax.dynamic_index_in_dim(arrived, (ctx_rank - m) % ratio, 0, keepdims=False)
            for m in range(ratio)
        ],
        axis=1,
    )
    outs = pl.pallas_call(
        finish_kernel,
        grid=(ctx_size // GROUP,),
        out_shape=(jax.ShapeDtypeStruct(queries.shape, jnp.bfloat16),) * 4,
        in_specs=[packed_spec] + [wide] * 4,
        out_specs=(wide,) * 4,
    )(back, queries, keys, values, cotangent)
    return (*outs, grad_filter)


def solution(mesh):
    in_specs = (
        P("dp", "ctx", None),
        P("dp", "ctx", None),
        P("dp", "ctx", None),
        P("dp", "ctx", None),
        P("dp", None),
        P("ctx", None),
    )
    out_specs = (
        P("dp", "ctx", None),
        P("dp", "ctx", None),
        P("dp", "ctx", None),
        P("dp", "ctx", None),
        P("ctx", "dp"),
    )
    return jax.shard_map(body, mesh=mesh, in_specs=in_specs, out_specs=out_specs, check_vma=False)
```

```python
import functools
import math

import jax
import jax.numpy as jnp
import numpy as np
import ml_dtypes
from jax import lax
from jax.experimental import pallas as pl
from jax.experimental.pallas import tpu as pltpu
from jax.sharding import PartitionSpec as P


def tables(block_len):
    turns = (2 * np.arange(block_len)[:, None] + 1) * np.arange(block_len)[None, :]
    angle = (turns % (4 * block_len)) * (2.0 * math.pi / (4 * block_len))
    forward = np.concatenate([np.cos(angle), -np.sin(angle)], axis=0)
    inverse = forward.T / block_len

    def split(table):
        high = table.astype(ml_dtypes.bfloat16)
        low = (table - high.astype(np.float64)).astype(ml_dtypes.bfloat16)
        return high, low

    fwd_high, fwd_low = split(forward)
    inv_high, inv_low = split(inverse)
    return (
        np.concatenate([fwd_high, fwd_low], axis=1),
        np.concatenate([inv_high, inv_high, inv_low], axis=1),
    )


def conv_kernel(
    lengths_ref, rows_ref, taps_ref, fwd_ref, inv_ref, conv_ref, lag_ref,
    in_spec, wt_spec, filt_spec, conv_spec, adj_spec, lag_spec, conv_acc, adj_acc,
):
    blocks, double, channels = in_spec.shape
    block_len = double // 2
    docs = lengths_ref.shape[1]
    row_id = lax.broadcasted_iota(jnp.int32, (block_len, channels), 0)
    sign = (1 - 2 * (row_id % 2)).astype(jnp.float32)
    chunk = 16

    def rows_at(block):
        return pl.ds(pl.multiple_of(block * block_len, block_len), block_len)

    def forward(rows):
        return jnp.dot(
            fwd_ref[...], jnp.concatenate([rows, rows], axis=0), preferred_element_type=jnp.float32
        )

    def inverse(spec):
        high = spec.astype(jnp.bfloat16)
        low = (spec - high.astype(jnp.float32)).astype(jnp.bfloat16)
        return jnp.dot(
            inv_ref[...], jnp.concatenate([high, low, high], axis=0),
            preferred_element_type=jnp.float32,
        )

    @pl.loop(0, blocks)
    def _(block):
        taps = [taps_ref[part, block] for part in range(taps_ref.shape[0])]
        adj_spec[block] = forward(jnp.concatenate(taps, axis=0))
        lag_spec[block] = jnp.zeros((double, channels), jnp.float32)

    filt_spec[0] = adj_spec[0]

    @pl.loop(1, blocks)
    def _(block):
        filt_spec[block, :block_len] = (
            adj_spec[block, :block_len] - sign * adj_spec[block - 1, block_len:]
        )
        filt_spec[block, block_len:] = (
            adj_spec[block, block_len:] + sign * adj_spec[block - 1, :block_len]
        )

    conv_acc[...] = jnp.zeros_like(conv_acc)
    adj_acc[...] = jnp.zeros_like(adj_acc)

    def doc_work(doc, start):
        length = lengths_ref[0, doc]
        end = start + length
        low_block = start // block_len
        high_block = jnp.where(length > 0, (end + block_len - 1) // block_len, low_block)

        def keep(block):
            pos = row_id + block * block_len
            return (pos >= start) & (pos < end)

        @pl.loop(low_block, high_block)
        def _(block):
            kept = keep(block)

            def masked(which):
                rows = rows_ref[block, which].astype(jnp.float32)
                return jnp.where(kept, rows, 0.0).astype(jnp.bfloat16)

            in_spec[block] = forward(masked(0))
            wt_spec[block] = forward(masked(1))
            conv_spec[block] = jnp.zeros((double, channels), jnp.float32)
            adj_spec[block] = jnp.zeros((double, channels), jnp.float32)

        @pl.loop(low_block, high_block)
        def _(target):
            @pl.loop(low_block, target + 1)
            def _(source):
                lag = target - source
                for base in range(0, block_len, chunk):
                    re = pl.ds(base, chunk)
                    im = pl.ds(base + block_len, chunk)
                    filt_re, filt_im = filt_spec[lag, re], filt_spec[lag, im]
                    in_re, in_im = in_spec[source, re], in_spec[source, im]
                    wt_re, wt_im = wt_spec[target, re], wt_spec[target, im]
                    conv_spec[target, re] += filt_re * in_re - filt_im * in_im
                    conv_spec[target, im] += filt_re * in_im + filt_im * in_re
                    adj_spec[source, re] += filt_re * wt_re + filt_im * wt_im
                    adj_spec[source, im] += filt_re * wt_im - filt_im * wt_re
                    lag_spec[lag, re] += wt_re * in_re + wt_im * in_im
                    lag_spec[lag, im] += wt_im * in_re - wt_re * in_im

        @pl.loop(low_block, high_block)
        def _(block):
            kept = keep(block)
            conv_acc[rows_at(block), :] += jnp.where(kept, inverse(conv_spec[block]), 0.0)
            adj_acc[rows_at(block), :] += jnp.where(kept, inverse(adj_spec[block]), 0.0)

        return end

    lax.fori_loop(0, docs, doc_work, jnp.int32(0))

    @pl.loop(0, blocks)
    def _(block):
        conv_ref[block, 0] = conv_acc[rows_at(block), :].astype(jnp.bfloat16)
        conv_ref[block, 1] = adj_acc[rows_at(block), :].astype(jnp.bfloat16)

    @pl.loop(0, blocks - 1)
    def _(block):
        real = lag_spec[block, :block_len] + sign * lag_spec[block + 1, block_len:]
        imag = lag_spec[block, block_len:] - sign * lag_spec[block + 1, :block_len]
        lag_ref[rows_at(block), :] = inverse(jnp.concatenate([real, imag], axis=0))

    lag_ref[rows_at(blocks - 1), :] = inverse(lag_spec[blocks - 1])


def local_conv(lengths, rows, taps):
    blocks, _, block_len, channels = rows.shape
    seq = blocks * block_len
    fwd_table, inv_table = tables(block_len)
    spec = pltpu.VMEM((blocks, 2 * block_len, channels), jnp.float32)
    vmem = pl.BlockSpec(memory_space=pltpu.VMEM)
    return pl.pallas_call(
        conv_kernel,
        out_shape=(
            jax.ShapeDtypeStruct(rows.shape, jnp.bfloat16),
            jax.ShapeDtypeStruct((seq, channels), jnp.float32),
        ),
        in_specs=[pl.BlockSpec(memory_space=pltpu.SMEM), vmem, vmem, vmem, vmem],
        out_specs=(vmem, vmem),
        scratch_shapes=[spec] * 6 + [pltpu.VMEM((seq, channels), jnp.float32)] * 2,
        compiler_params=pltpu.CompilerParams(vmem_limit_bytes=40 * 1024 * 1024),
    )(lengths, rows, taps, jnp.asarray(fwd_table), jnp.asarray(inv_table))


GROUP = 2


def gate_kernel(query_ref, key_ref, value_ref, cot_ref, out_ref):
    channels = out_ref.shape[3]
    for part in range(GROUP):
        cols = pl.ds(part * channels, channels)

        def load(ref):
            return ref[0, :, cols].astype(jnp.float32)

        out_ref[part, 0] = (load(key_ref) * load(value_ref)).astype(jnp.bfloat16)
        out_ref[part, 1] = (load(cot_ref) * load(query_ref)).astype(jnp.bfloat16)


def finish_kernel(
    back_ref, query_ref, key_ref, value_ref, cot_ref, out_ref, dquery_ref, dkey_ref, dvalue_ref
):
    channels = back_ref.shape[3]
    for part in range(GROUP):
        cols = pl.ds(part * channels, channels)

        def load(ref):
            return ref[0, :, cols].astype(jnp.float32)

        conv_rows = back_ref[part, 0].astype(jnp.float32)
        adj_rows = back_ref[part, 1].astype(jnp.float32)
        out_ref[0, :, cols] = (load(query_ref) * conv_rows).astype(jnp.bfloat16)
        dquery_ref[0, :, cols] = (load(cot_ref) * conv_rows).astype(jnp.bfloat16)
        dkey_ref[0, :, cols] = (adj_rows * load(value_ref)).astype(jnp.bfloat16)
        dvalue_ref[0, :, cols] = (adj_rows * load(key_ref)).astype(jnp.bfloat16)


def body(queries, keys, values, cotangent, doc_lengths, filter_taps):
    block_len, width = queries.shape[1:]
    ctx_size = lax.axis_size("ctx")
    dp_size = lax.axis_size("dp")
    ratio = ctx_size // dp_size
    ctx_rank = lax.axis_index("ctx")
    channels = width // ctx_size
    wide = pl.BlockSpec((1, block_len, GROUP * channels), lambda i: (0, 0, i))
    packed_spec = pl.BlockSpec((GROUP, 2, block_len, channels), lambda i: (i, 0, 0, 0))
    share = block_len // dp_size
    piece = lax.dynamic_slice_in_dim(filter_taps, lax.axis_index("dp") * share, share, 0)
    piece = piece.astype(jnp.bfloat16).reshape(share, ctx_size, channels).transpose(1, 0, 2)
    packed = pl.pallas_call(
        gate_kernel,
        grid=(ctx_size // GROUP,),
        out_shape=jax.ShapeDtypeStruct((ctx_size, 2, block_len, channels), jnp.bfloat16),
        in_specs=[wide] * 4,
        out_specs=packed_spec,
    )(queries, keys, values, cotangent)
    packed, piece = lax.optimization_barrier((packed, piece))
    rows = lax.all_to_all(packed, "ctx", split_axis=0, concat_axis=0, tiled=True)
    piece = lax.all_to_all(piece, "ctx", split_axis=0, concat_axis=0, tiled=True)
    taps = lax.all_gather(piece, "dp", axis=0, tiled=False)
    both, lags = local_conv(doc_lengths, rows, taps)
    back = lax.all_to_all(both, "ctx", split_axis=0, concat_axis=0, tiled=True)
    lag_share = lax.psum_scatter(lags, "dp", scatter_dimension=0, tiled=True)
    lag_share = lag_share.reshape(ratio, block_len, -1)
    arrived = []
    for step in range(ratio):
        pairs = [
            (d * ctx_size + c, (c // ratio) * ctx_size + ratio * d + (c + step) % ratio)
            for d in range(dp_size)
            for c in range(ctx_size)
        ]
        piece = lax.dynamic_index_in_dim(lag_share, (ctx_rank + step) % ratio, 0, keepdims=False)
        arrived.append(lax.ppermute(piece, ("dp", "ctx"), pairs))
    arrived = jnp.stack(arrived)
    grad_filter = jnp.concatenate(
        [
            lax.dynamic_index_in_dim(arrived, (ctx_rank - m) % ratio, 0, keepdims=False)
            for m in range(ratio)
        ],
        axis=1,
    )
    outs = pl.pallas_call(
        finish_kernel,
        grid=(ctx_size // GROUP,),
        out_shape=(jax.ShapeDtypeStruct(queries.shape, jnp.bfloat16),) * 4,
        in_specs=[packed_spec] + [wide] * 4,
        out_specs=(wide,) * 4,
    )(back, queries, keys, values, cotangent)
    return (*outs, grad_filter)


def solution(mesh):
    in_specs = (
        P("dp", "ctx", None),
        P("dp", "ctx", None),
        P("dp", "ctx", None),
        P("dp", "ctx", None),
        P("dp", None),
        P("ctx", None),
    )
    out_specs = (
        P("dp", "ctx", None),
        P("dp", "ctx", None),
        P("dp", "ctx", None),
        P("dp", "ctx", None),
        P("ctx", "dp"),
    )
    return jax.shard_map(body, mesh=mesh, in_specs=in_specs, out_specs=out_specs, check_vma=False)
```

```python
import functools
import math

import jax
import jax.numpy as jnp
import numpy as np
import ml_dtypes
from jax import lax
from jax.experimental import pallas as pl
from jax.experimental.pallas import tpu as pltpu
from jax.sharding import PartitionSpec as P


def tables(block_len):
    turns = (2 * np.arange(block_len)[:, None] + 1) * np.arange(block_len)[None, :]
    angle = (turns % (4 * block_len)) * (2.0 * math.pi / (4 * block_len))
    forward = np.concatenate([np.cos(angle), -np.sin(angle)], axis=0)
    inverse = forward.T / block_len

    def split(table):
        high = table.astype(ml_dtypes.bfloat16)
        low = (table - high.astype(np.float64)).astype(ml_dtypes.bfloat16)
        return high, low

    fwd_high, fwd_low = split(forward)
    inv_high, inv_low = split(inverse)
    return (
        np.concatenate([fwd_high, fwd_low], axis=1),
        np.concatenate([inv_high, inv_high, inv_low], axis=1),
    )


def conv_kernel(
    lengths_ref, rows_ref, taps_ref, fwd_ref, inv_ref, conv_ref, lag_ref,
    in_spec, wt_spec, filt_spec, conv_spec, adj_spec, lag_spec, conv_acc, adj_acc,
):
    blocks, double, channels = in_spec.shape
    block_len = double // 2
    docs = lengths_ref.shape[1]
    row_id = lax.broadcasted_iota(jnp.int32, (block_len, channels), 0)
    sign = (1 - 2 * (row_id % 2)).astype(jnp.float32)
    chunk = 16

    def rows_at(block):
        return pl.ds(pl.multiple_of(block * block_len, block_len), block_len)

    def forward(rows):
        return jnp.dot(
            fwd_ref[...], jnp.concatenate([rows, rows], axis=0), preferred_element_type=jnp.float32
        )

    def inverse(spec):
        high = spec.astype(jnp.bfloat16)
        low = (spec - high.astype(jnp.float32)).astype(jnp.bfloat16)
        return jnp.dot(
            inv_ref[...], jnp.concatenate([high, low, high], axis=0),
            preferred_element_type=jnp.float32,
        )

    @pl.loop(0, blocks)
    def _(block):
        taps = [taps_ref[part, block] for part in range(taps_ref.shape[0])]
        adj_spec[block] = forward(jnp.concatenate(taps, axis=0))
        lag_spec[block] = jnp.zeros((double, channels), jnp.float32)

    filt_spec[0] = adj_spec[0]

    @pl.loop(1, blocks)
    def _(block):
        filt_spec[block, :block_len] = (
            adj_spec[block, :block_len] - sign * adj_spec[block - 1, block_len:]
        )
        filt_spec[block, block_len:] = (
            adj_spec[block, block_len:] + sign * adj_spec[block - 1, :block_len]
        )

    conv_acc[...] = jnp.zeros_like(conv_acc)
    adj_acc[...] = jnp.zeros_like(adj_acc)

    def doc_work(doc, start):
        length = lengths_ref[0, doc]
        end = start + length
        low_block = start // block_len
        high_block = jnp.where(length > 0, (end + block_len - 1) // block_len, low_block)

        def keep(block):
            pos = row_id + block * block_len
            return (pos >= start) & (pos < end)

        @pl.loop(low_block, high_block)
        def _(block):
            kept = keep(block)

            def masked(which):
                rows = rows_ref[block, which].astype(jnp.float32)
                return jnp.where(kept, rows, 0.0).astype(jnp.bfloat16)

            in_spec[block] = forward(masked(0))
            wt_spec[block] = forward(masked(1))
            conv_spec[block] = jnp.zeros((double, channels), jnp.float32)
            adj_spec[block] = jnp.zeros((double, channels), jnp.float32)

        @pl.loop(low_block, high_block)
        def _(target):
            @pl.loop(low_block, target + 1)
            def _(source):
                lag = target - source
                for base in range(0, block_len, chunk):
                    re = pl.ds(base, chunk)
                    im = pl.ds(base + block_len, chunk)
                    filt_re, filt_im = filt_spec[lag, re], filt_spec[lag, im]
                    in_re, in_im = in_spec[source, re], in_spec[source, im]
                    wt_re, wt_im = wt_spec[target, re], wt_spec[target, im]
                    conv_spec[target, re] += filt_re * in_re - filt_im * in_im
                    conv_spec[target, im] += filt_re * in_im + filt_im * in_re
                    adj_spec[source, re] += filt_re * wt_re + filt_im * wt_im
                    adj_spec[source, im] += filt_re * wt_im - filt_im * wt_re
                    lag_spec[lag, re] += wt_re * in_re + wt_im * in_im
                    lag_spec[lag, im] += wt_im * in_re - wt_re * in_im

        @pl.loop(low_block, high_block)
        def _(block):
            kept = keep(block)
            conv_acc[rows_at(block), :] += jnp.where(kept, inverse(conv_spec[block]), 0.0)
            adj_acc[rows_at(block), :] += jnp.where(kept, inverse(adj_spec[block]), 0.0)

        return end

    lax.fori_loop(0, docs, doc_work, jnp.int32(0))

    @pl.loop(0, blocks)
    def _(block):
        conv_ref[block, 0] = conv_acc[rows_at(block), :].astype(jnp.bfloat16)
        conv_ref[block, 1] = adj_acc[rows_at(block), :].astype(jnp.bfloat16)

    @pl.loop(0, blocks - 1)
    def _(block):
        real = lag_spec[block, :block_len] + sign * lag_spec[block + 1, block_len:]
        imag = lag_spec[block, block_len:] - sign * lag_spec[block + 1, :block_len]
        lag_ref[rows_at(block), :] = inverse(jnp.concatenate([real, imag], axis=0))

    lag_ref[rows_at(blocks - 1), :] = inverse(lag_spec[blocks - 1])


def local_conv(lengths, rows, taps):
    blocks, _, block_len, channels = rows.shape
    seq = blocks * block_len
    fwd_table, inv_table = tables(block_len)
    spec = pltpu.VMEM((blocks, 2 * block_len, channels), jnp.float32)
    vmem = pl.BlockSpec(memory_space=pltpu.VMEM)
    return pl.pallas_call(
        conv_kernel,
        out_shape=(
            jax.ShapeDtypeStruct(rows.shape, jnp.bfloat16),
            jax.ShapeDtypeStruct((seq, channels), jnp.float32),
        ),
        in_specs=[pl.BlockSpec(memory_space=pltpu.SMEM), vmem, vmem, vmem, vmem],
        out_specs=(vmem, vmem),
        scratch_shapes=[spec] * 6 + [pltpu.VMEM((seq, channels), jnp.float32)] * 2,
        compiler_params=pltpu.CompilerParams(vmem_limit_bytes=40 * 1024 * 1024),
    )(lengths, rows, taps, jnp.asarray(fwd_table), jnp.asarray(inv_table))


def gate_kernel(query_ref, key_ref, value_ref, cot_ref, out_ref):
    blocks, _, _, channels = out_ref.shape
    for part in range(blocks):
        cols = pl.ds(part * channels, channels)

        def load(ref):
            return ref[0, :, cols].astype(jnp.float32)

        out_ref[part, 0] = (load(key_ref) * load(value_ref)).astype(jnp.bfloat16)
        out_ref[part, 1] = (load(cot_ref) * load(query_ref)).astype(jnp.bfloat16)


def finish_kernel(
    back_ref, query_ref, key_ref, value_ref, cot_ref, out_ref, dquery_ref, dkey_ref, dvalue_ref
):
    blocks, _, _, channels = back_ref.shape
    for part in range(blocks):
        cols = pl.ds(part * channels, channels)

        def load(ref):
            return ref[0, :, cols].astype(jnp.float32)

        conv_rows = back_ref[part, 0].astype(jnp.float32)
        adj_rows = back_ref[part, 1].astype(jnp.float32)
        out_ref[0, :, cols] = (load(query_ref) * conv_rows).astype(jnp.bfloat16)
        dquery_ref[0, :, cols] = (load(cot_ref) * conv_rows).astype(jnp.bfloat16)
        dkey_ref[0, :, cols] = (adj_rows * load(value_ref)).astype(jnp.bfloat16)
        dvalue_ref[0, :, cols] = (adj_rows * load(key_ref)).astype(jnp.bfloat16)


def body(queries, keys, values, cotangent, doc_lengths, filter_taps):
    block_len, width = queries.shape[1:]
    ctx_size = lax.axis_size("ctx")
    dp_size = lax.axis_size("dp")
    ratio = ctx_size // dp_size
    ctx_rank = lax.axis_index("ctx")
    channels = width // ctx_size
    vmem = pl.BlockSpec(memory_space=pltpu.VMEM)
    params = pltpu.CompilerParams(vmem_limit_bytes=16 * 1024 * 1024)
    share = block_len // dp_size
    piece = lax.dynamic_slice_in_dim(filter_taps, lax.axis_index("dp") * share, share, 0)
    piece = piece.astype(jnp.bfloat16).reshape(share, ctx_size, channels).transpose(1, 0, 2)
    piece = lax.all_to_all(piece, "ctx", split_axis=0, concat_axis=0, tiled=True)
    packed = pl.pallas_call(
        gate_kernel,
        out_shape=jax.ShapeDtypeStruct((ctx_size, 2, block_len, channels), jnp.bfloat16),
        in_specs=[vmem] * 4,
        out_specs=vmem,
        compiler_params=params,
    )(queries, keys, values, cotangent)
    packed, piece = lax.optimization_barrier((packed, piece))
    taps = lax.all_gather(piece, "dp", axis=0, tiled=False)
    rows = lax.all_to_all(packed, "ctx", split_axis=0, concat_axis=0, tiled=True)
    both, lags = local_conv(doc_lengths, rows, taps)
    back = lax.all_to_all(both, "ctx", split_axis=0, concat_axis=0, tiled=True)
    lag_share = lax.psum_scatter(lags, "dp", scatter_dimension=0, tiled=True)
    lag_share = lag_share.reshape(ratio, block_len, -1)
    arrived = []
    for step in range(ratio):
        pairs = [
            (d * ctx_size + c, (c // ratio) * ctx_size + ratio * d + (c + step) % ratio)
            for d in range(dp_size)
            for c in range(ctx_size)
        ]
        piece = lax.dynamic_index_in_dim(lag_share, (ctx_rank + step) % ratio, 0, keepdims=False)
        arrived.append(lax.ppermute(piece, ("dp", "ctx"), pairs))
    arrived = jnp.stack(arrived)
    grad_filter = jnp.concatenate(
        [
            lax.dynamic_index_in_dim(arrived, (ctx_rank - m) % ratio, 0, keepdims=False)
            for m in range(ratio)
        ],
        axis=1,
    )
    outs = pl.pallas_call(
        finish_kernel,
        out_shape=(jax.ShapeDtypeStruct(queries.shape, jnp.bfloat16),) * 4,
        in_specs=[vmem] * 5,
        out_specs=(vmem,) * 4,
        compiler_params=params,
    )(back, queries, keys, values, cotangent)
    return (*outs, grad_filter)


def solution(mesh):
    in_specs = (
        P("dp", "ctx", None),
        P("dp", "ctx", None),
        P("dp", "ctx", None),
        P("dp", "ctx", None),
        P("dp", None),
        P("ctx", None),
    )
    out_specs = (
        P("dp", "ctx", None),
        P("dp", "ctx", None),
        P("dp", "ctx", None),
        P("dp", "ctx", None),
        P("ctx", "dp"),
    )
    return jax.shard_map(body, mesh=mesh, in_specs=in_specs, out_specs=out_specs, check_vma=False)
```

```python
import functools
import math

import jax
import jax.numpy as jnp
import numpy as np
import ml_dtypes
from jax import lax
from jax.experimental import pallas as pl
from jax.experimental.pallas import tpu as pltpu
from jax.sharding import PartitionSpec as P


def tables(block_len):
    turns = (2 * np.arange(block_len)[:, None] + 1) * np.arange(block_len)[None, :]
    angle = (turns % (4 * block_len)) * (2.0 * math.pi / (4 * block_len))
    forward = np.concatenate([np.cos(angle), -np.sin(angle)], axis=0)
    inverse = forward.T / block_len

    def split(table):
        high = table.astype(ml_dtypes.bfloat16)
        low = (table - high.astype(np.float64)).astype(ml_dtypes.bfloat16)
        return high, low

    fwd_high, fwd_low = split(forward)
    inv_high, inv_low = split(inverse)
    return (
        np.concatenate([fwd_high, fwd_low], axis=1),
        np.concatenate([inv_high, inv_high, inv_low], axis=1),
    )


def conv_kernel(
    lengths_ref, rows_ref, taps_ref, fwd_ref, inv_ref, conv_ref, lag_ref,
    in_spec, wt_spec, filt_spec, conv_spec, adj_spec, lag_spec, conv_acc, adj_acc,
):
    blocks, double, channels = in_spec.shape
    block_len = double // 2
    docs = lengths_ref.shape[1]
    row_id = lax.broadcasted_iota(jnp.int32, (block_len, channels), 0)
    sign = (1 - 2 * (row_id % 2)).astype(jnp.float32)
    chunk = 16

    def rows_at(block):
        return pl.ds(pl.multiple_of(block * block_len, block_len), block_len)

    def forward(rows):
        return jnp.dot(
            fwd_ref[...], jnp.concatenate([rows, rows], axis=0), preferred_element_type=jnp.float32
        )

    def inverse(spec):
        high = spec.astype(jnp.bfloat16)
        low = (spec - high.astype(jnp.float32)).astype(jnp.bfloat16)
        return jnp.dot(
            inv_ref[...], jnp.concatenate([high, low, high], axis=0),
            preferred_element_type=jnp.float32,
        )

    @pl.loop(0, blocks)
    def _(block):
        taps = [taps_ref[part, block] for part in range(taps_ref.shape[0])]
        adj_spec[block] = forward(jnp.concatenate(taps, axis=0))
        lag_spec[block] = jnp.zeros((double, channels), jnp.float32)

    filt_spec[0] = adj_spec[0]

    @pl.loop(1, blocks)
    def _(block):
        filt_spec[block, :block_len] = (
            adj_spec[block, :block_len] - sign * adj_spec[block - 1, block_len:]
        )
        filt_spec[block, block_len:] = (
            adj_spec[block, block_len:] + sign * adj_spec[block - 1, :block_len]
        )

    conv_acc[...] = jnp.zeros_like(conv_acc)
    adj_acc[...] = jnp.zeros_like(adj_acc)

    def doc_work(doc, start):
        length = lengths_ref[0, doc]
        end = start + length
        low_block = start // block_len
        high_block = jnp.where(length > 0, (end + block_len - 1) // block_len, low_block)

        def keep(block):
            pos = row_id + block * block_len
            return (pos >= start) & (pos < end)

        @pl.loop(low_block, high_block)
        def _(block):
            kept = keep(block)

            def masked(which):
                rows = rows_ref[block, which].astype(jnp.float32)
                return jnp.where(kept, rows, 0.0).astype(jnp.bfloat16)

            in_spec[block] = forward(masked(0))
            wt_spec[block] = forward(masked(1))
            conv_spec[block] = jnp.zeros((double, channels), jnp.float32)
            adj_spec[block] = jnp.zeros((double, channels), jnp.float32)

        @pl.loop(low_block, high_block)
        def _(target):
            @pl.loop(low_block, target + 1)
            def _(source):
                lag = target - source
                for base in range(0, block_len, chunk):
                    re = pl.ds(base, chunk)
                    im = pl.ds(base + block_len, chunk)
                    filt_re, filt_im = filt_spec[lag, re], filt_spec[lag, im]
                    in_re, in_im = in_spec[source, re], in_spec[source, im]
                    wt_re, wt_im = wt_spec[target, re], wt_spec[target, im]
                    conv_spec[target, re] += filt_re * in_re - filt_im * in_im
                    conv_spec[target, im] += filt_re * in_im + filt_im * in_re
                    adj_spec[source, re] += filt_re * wt_re + filt_im * wt_im
                    adj_spec[source, im] += filt_re * wt_im - filt_im * wt_re
                    lag_spec[lag, re] += wt_re * in_re + wt_im * in_im
                    lag_spec[lag, im] += wt_im * in_re - wt_re * in_im

        @pl.loop(low_block, high_block)
        def _(block):
            kept = keep(block)
            conv_acc[rows_at(block), :] += jnp.where(kept, inverse(conv_spec[block]), 0.0)
            adj_acc[rows_at(block), :] += jnp.where(kept, inverse(adj_spec[block]), 0.0)

        return end

    lax.fori_loop(0, docs, doc_work, jnp.int32(0))

    @pl.loop(0, blocks)
    def _(block):
        conv_ref[block, 0] = conv_acc[rows_at(block), :].astype(jnp.bfloat16)
        conv_ref[block, 1] = adj_acc[rows_at(block), :].astype(jnp.bfloat16)

    @pl.loop(0, blocks - 1)
    def _(block):
        real = lag_spec[block, :block_len] + sign * lag_spec[block + 1, block_len:]
        imag = lag_spec[block, block_len:] - sign * lag_spec[block + 1, :block_len]
        total = inverse(jnp.concatenate([real, imag], axis=0))
        lag_ref[rows_at(block), :] = total.astype(jnp.bfloat16)

    lag_ref[rows_at(blocks - 1), :] = inverse(lag_spec[blocks - 1]).astype(jnp.bfloat16)


def local_conv(lengths, rows, taps):
    blocks, _, block_len, channels = rows.shape
    seq = blocks * block_len
    fwd_table, inv_table = tables(block_len)
    spec = pltpu.VMEM((blocks, 2 * block_len, channels), jnp.float32)
    vmem = pl.BlockSpec(memory_space=pltpu.VMEM)
    return pl.pallas_call(
        conv_kernel,
        out_shape=(
            jax.ShapeDtypeStruct(rows.shape, jnp.bfloat16),
            jax.ShapeDtypeStruct((seq, channels), jnp.bfloat16),
        ),
        in_specs=[pl.BlockSpec(memory_space=pltpu.SMEM), vmem, vmem, vmem, vmem],
        out_specs=(vmem, vmem),
        scratch_shapes=[spec] * 6 + [pltpu.VMEM((seq, channels), jnp.float32)] * 2,
        compiler_params=pltpu.CompilerParams(vmem_limit_bytes=40 * 1024 * 1024),
    )(lengths, rows, taps, jnp.asarray(fwd_table), jnp.asarray(inv_table))


GROUP = 2


def gate_kernel(query_ref, key_ref, value_ref, cot_ref, out_ref):
    channels = out_ref.shape[3]
    for part in range(GROUP):
        cols = pl.ds(part * channels, channels)

        def load(ref):
            return ref[0, :, cols].astype(jnp.float32)

        out_ref[part, 0] = (load(key_ref) * load(value_ref)).astype(jnp.bfloat16)
        out_ref[part, 1] = (load(cot_ref) * load(query_ref)).astype(jnp.bfloat16)


def finish_kernel(
    back_ref, query_ref, key_ref, value_ref, cot_ref, out_ref, dquery_ref, dkey_ref, dvalue_ref
):
    channels = back_ref.shape[3]
    for part in range(GROUP):
        cols = pl.ds(part * channels, channels)

        def load(ref):
            return ref[0, :, cols].astype(jnp.float32)

        conv_rows = back_ref[part, 0].astype(jnp.float32)
        adj_rows = back_ref[part, 1].astype(jnp.float32)
        out_ref[0, :, cols] = (load(query_ref) * conv_rows).astype(jnp.bfloat16)
        dquery_ref[0, :, cols] = (load(cot_ref) * conv_rows).astype(jnp.bfloat16)
        dkey_ref[0, :, cols] = (adj_rows * load(value_ref)).astype(jnp.bfloat16)
        dvalue_ref[0, :, cols] = (adj_rows * load(key_ref)).astype(jnp.bfloat16)


def body(queries, keys, values, cotangent, doc_lengths, filter_taps):
    block_len, width = queries.shape[1:]
    ctx_size = lax.axis_size("ctx")
    dp_size = lax.axis_size("dp")
    ratio = ctx_size // dp_size
    ctx_rank = lax.axis_index("ctx")
    channels = width // ctx_size
    wide = pl.BlockSpec((1, block_len, GROUP * channels), lambda i: (0, 0, i))
    packed_spec = pl.BlockSpec((GROUP, 2, block_len, channels), lambda i: (i, 0, 0, 0))
    share = block_len // dp_size
    piece = lax.dynamic_slice_in_dim(filter_taps, lax.axis_index("dp") * share, share, 0)
    piece = piece.astype(jnp.bfloat16).reshape(share, ctx_size, channels).transpose(1, 0, 2)
    piece = lax.all_to_all(piece, "ctx", split_axis=0, concat_axis=0, tiled=True)
    packed = pl.pallas_call(
        gate_kernel,
        grid=(ctx_size // GROUP,),
        out_shape=jax.ShapeDtypeStruct((ctx_size, 2, block_len, channels), jnp.bfloat16),
        in_specs=[wide] * 4,
        out_specs=packed_spec,
    )(queries, keys, values, cotangent)
    packed, piece = lax.optimization_barrier((packed, piece))
    taps = lax.all_gather(piece, "dp", axis=0, tiled=False)
    rows = lax.all_to_all(packed, "ctx", split_axis=0, concat_axis=0, tiled=True)
    both, lags = local_conv(doc_lengths, rows, taps)
    back = lax.all_to_all(both, "ctx", split_axis=0, concat_axis=0, tiled=True)
    lag_share = lax.psum_scatter(lags, "dp", scatter_dimension=0, tiled=True)
    lag_share = lag_share.reshape(ratio, block_len, -1)
    arrived = []
    for step in range(ratio):
        pairs = [
            (d * ctx_size + c, (c // ratio) * ctx_size + ratio * d + (c + step) % ratio)
            for d in range(dp_size)
            for c in range(ctx_size)
        ]
        piece = lax.dynamic_index_in_dim(lag_share, (ctx_rank + step) % ratio, 0, keepdims=False)
        arrived.append(lax.ppermute(piece, ("dp", "ctx"), pairs))
    arrived = jnp.stack(arrived)
    grad_filter = jnp.concatenate(
        [
            lax.dynamic_index_in_dim(arrived, (ctx_rank - m) % ratio, 0, keepdims=False)
            for m in range(ratio)
        ],
        axis=1,
    ).astype(jnp.float32)
    outs = pl.pallas_call(
        finish_kernel,
        grid=(ctx_size // GROUP,),
        out_shape=(jax.ShapeDtypeStruct(queries.shape, jnp.bfloat16),) * 4,
        in_specs=[packed_spec] + [wide] * 4,
        out_specs=(wide,) * 4,
    )(back, queries, keys, values, cotangent)
    return (*outs, grad_filter)


def solution(mesh):
    in_specs = (
        P("dp", "ctx", None),
        P("dp", "ctx", None),
        P("dp", "ctx", None),
        P("dp", "ctx", None),
        P("dp", None),
        P("ctx", None),
    )
    out_specs = (
        P("dp", "ctx", None),
        P("dp", "ctx", None),
        P("dp", "ctx", None),
        P("dp", "ctx", None),
        P("ctx", "dp"),
    )
    return jax.shard_map(body, mesh=mesh, in_specs=in_specs, out_specs=out_specs, check_vma=False)
```
